512 devices in a mesh: seq: 64 (over x, z_lo, y), chan: 8 (over z_hi, core).
Axes of the slice: x: 4, y: 8, z: 8 (z_hi: 4, z_lo: 2; z = z_hi * 2 + z_lo), core: 2. Of those that a mesh axis runs over, the one named last changes fastest.
Arguments:
- token_ids: int32 [8192], P('seq'), may hold values from 0 to 511
- vocab_table: bfloat16 [512, 4, 4096], P(None, None, 'chan'), may hold values from -6 to 6
- short_taps: bfloat16 [3, 3, 4096], P(None, None, 'chan'), may hold values from -3 to 3
- filter_spec: bfloat16 [2, 128, 128, 4096], P(None, 'seq', None, 'chan'), may hold values from -6 to 6
- out_weight: bfloat16 [4096, 4096], P('chan', 'seq'), may hold values from -0.25 to 0.25
Outputs:
- mixed: bfloat16 [8192, 4096], P('seq', 'chan')
- gated: bfloat16 [8192, 4096], P('seq', 'chan')
The draws below stay inside these ranges and needn't reach their ends.
All inputs are finite; a program needn't handle non-finite values.
Results may differ from the reference program's by a relative error of at most 0.02.
Values may be sent and summed in bfloat16 or wider, within the bound.
A program may use at most 64 MiB of HBM per device.

```python
import math
import jax
import jax.numpy as jnp
import numpy as np
from jax import lax

D = 4096
VOCAB = 512
TOK_DEV = 128
TOKENS = 8192
N_SEQ = 64
N_CHAN = 8


def with_ends(array, key, low, high):
    longest = array.shape.index(max(array.shape))
    spots = []
    for shift in (0, 1):
        where = [jax.random.randint(jax.random.fold_in(key, axis), (), 0, length) for axis, length in enumerate(array.shape)]
        where[longest] = (where[longest] + shift) % array.shape[longest]
        spots.append(tuple(where))
    return array.at[spots[0]].set(low).at[spots[1]].set(high)


def with_spikes(values, own_key, source, target, blocks, factor):
    def block_of(position):
        return (jnp.arange(values.shape[position]) // (values.shape[position] // blocks)).reshape((-1,) + (1,) * (values.ndim - 1 - position))

    first = jax.random.permutation(own_key, blocks)[block_of(target)]
    other_side = (block_of(target) + blocks // 2) % blocks
    return jnp.where((block_of(source) == first) | (block_of(source) == other_side), factor * values, values)


def shard_levels(own_key, shape, split, low, high):
    loudness, own = 1.0, jax.random.fold_in(own_key, 6)
    for axis_at, blocks in split:
        steps = jnp.exp(jax.random.uniform(jax.random.fold_in(own, axis_at), (blocks,), jnp.float32, low / len(split), high / len(split)))
        loudness = loudness * jnp.repeat(steps, shape[axis_at] // blocks).reshape([-1 if axis == axis_at else 1 for axis in range(len(shape))])
    return loudness


def rank_bounds(number_of, lean):
    loads = [(1 << 20) // math.isqrt(grade ** lean) + 1 for grade in range(1, number_of + 1)]
    width = 1 + sum(loads) // (1 << 30)
    return np.cumsum(np.array([max(1, weight // width) for weight in loads]))


def ranked_ids(key, shape, count, lean):
    listing = rank_bounds(count, lean)
    ticket = jax.random.randint(jax.random.fold_in(key, 1), shape, 0, int(listing[count - 1]))
    standing = jnp.searchsorted(jnp.asarray(listing, jnp.int32), ticket, side="right")
    return jax.random.permutation(jax.random.fold_in(key, 2), count)[standing].astype(jnp.int32)


def gaussian(rng, shape, width, bound, pieces=(), kind=jnp.bfloat16):
    gain = shard_levels(rng, shape, pieces, -0.22, 0.18) if pieces else 1.0
    result = jax.random.normal(rng, shape, jnp.float32) * width * gain
    return jnp.minimum(jnp.maximum(result, -bound), bound).astype(kind)


def bell_draw_with(stream_key, dims, spread, reach, shards, heavy, held_as=jnp.bfloat16):
    entries = spread * jax.random.normal(stream_key, dims, jnp.float32)
    if shards:
        entries = entries * shard_levels(stream_key, dims, shards, -0.22, 0.18)
    return jnp.clip(with_spikes(entries, jax.random.fold_in(stream_key, 3), *heavy), -reach, reach).astype(held_as)


def setup_inputs(seed: int = 0) -> dict:
    key_list = jax.random.split(jax.random.key(seed), 6)
    token_ids = with_ends(ranked_ids(key_list[0], (TOKENS,), VOCAB, 2), jax.random.fold_in(key_list[0], 3), 0, VOCAB - 1).astype(jnp.int32)
    vocab_table = gaussian(key_list[1], (VOCAB, 4, D), 1.0, 6.0, ((2, 8),))
    short_taps = gaussian(key_list[2], (3, 3, D), 0.5, 3.0, ((2, 8),))
    filter_spec = gaussian(key_list[3], (2, 2 * N_SEQ, TOK_DEV, D), 1.0, 6.0, ((1, 64), (3, 8)))
    out_weight = bell_draw_with(key_list[4], (D, D), D ** -0.5, 0.25, ((0, 8), (1, 64)), (0, 1, 64, 4.0))
    return {"token_ids": token_ids, "vocab_table": vocab_table, "short_taps": short_taps, "filter_spec": filter_spec, "out_weight": out_weight}


def reference(token_ids, vocab_table, short_taps, filter_spec, out_weight):
    features = vocab_table[token_ids]
    extended = jnp.pad(features[:, :3, :].astype(jnp.float32), ((2, 0), (0, 0), (0, 0)))
    weights = short_taps.astype(jnp.float32)
    shortened = weights[:, 0] * extended[2:] + weights[:, 1] * extended[1:-1] + weights[:, 2] * extended[:-2]
    signal = (shortened[:, 1] * shortened[:, 2]).astype(jnp.bfloat16)
    block_width = 128
    block_count = D // block_width
    spectrum = jnp.transpose(filter_spec.astype(jnp.float32), (0, 2, 1, 3)).reshape(2, 2 * TOKENS, D)

    def convolve(index):
        start = index.astype(jnp.int32) * block_width
        columns = lax.dynamic_slice_in_dim(signal, start, block_width, 1).astype(jnp.float32)
        padded = jnp.pad(columns, ((0, TOKENS), (0, 0)))
        spec_real = lax.dynamic_slice_in_dim(spectrum[0], start, block_width, 1)
        spec_imag = lax.dynamic_slice_in_dim(spectrum[1], start, block_width, 1)
        product = jnp.fft.fft(padded, axis=0) * lax.complex(spec_real, spec_imag)
        return jnp.real(jnp.fft.ifft(product, axis=0))[:TOKENS]

    blocks = lax.map(convolve, jnp.arange(block_count, dtype=jnp.int32))
    conv = jnp.transpose(blocks, (1, 0, 2)).reshape(TOKENS, D)
    gated = (shortened[:, 0] * conv).astype(jnp.bfloat16)
    group_width = D // N_CHAN

    def accumulate(index, total):
        start = jnp.asarray(index).astype(jnp.int32) * group_width
        rows = lax.dynamic_slice_in_dim(gated, start, group_width, 1)
        weight_rows = lax.dynamic_slice_in_dim(out_weight, start, group_width, 0)
        term = jnp.dot(rows, weight_rows, preferred_element_type=jnp.float32)
        term = lax.optimization_barrier(term.astype(jnp.bfloat16)).astype(jnp.float32)
        return total + term

    summed = lax.fori_loop(0, N_CHAN, accumulate, jnp.zeros((TOKENS, D), jnp.float32))
    mixed = (features[:, 3, :].astype(jnp.float32) + summed).astype(jnp.bfloat16)
    return mixed, gated
```

```python
import jax
import jax.numpy as jnp
import numpy as np
from jax import lax
from jax.experimental import pallas as pl
from jax.experimental.pallas import tpu as pltpu
from jax.sharding import PartitionSpec as P

MESH = pl.DeviceIdType.MESH
F32 = jnp.float32
BF16 = jnp.bfloat16

NX, NZ, NY = 4, 2, 8
NH = 4
SEQ = NX * NZ * NY
TOK = 128
CH = 512
OWN = CH // SEQ
LEN = 2 * SEQ * TOK
FAR_FIRST = (4, 3, 5, 2, 6, 1, 7)


def tables():
    a = np.concatenate([np.arange(0, 128, 2), np.arange(1, 128, 2)])
    p = np.arange(SEQ)
    m = np.arange(TOK)
    t1 = 2 * np.pi * (np.outer(a, p) % 128) / 128
    first = np.concatenate([np.cos(t1), -np.sin(t1)], 0)
    hi = first.astype(jnp.bfloat16)
    lo = (first - hi.astype(np.float64)).astype(jnp.bfloat16)
    first = np.concatenate([hi, lo], 1)
    tw = 2 * np.pi * (np.outer(a, m) % LEN) / LEN
    twid = np.stack([np.cos(tw), np.sin(tw)]).astype(np.float32)
    t2 = 2 * np.pi * (np.outer(m, m) % 128) / 128
    c2, s2 = np.cos(t2), np.sin(t2)
    forward = np.block([[c2, -s2], [s2, c2]]).astype(jnp.bfloat16)
    inverse = np.block([[c2, s2], [-s2, c2]]).astype(jnp.bfloat16)
    last = (np.concatenate([np.cos(t1), -np.sin(t1)], 0).T / LEN).astype(jnp.bfloat16)
    return first, twid, forward, inverse, last


def kernel(
    ids, tab, taps, spec, wt, first, twid, forward, inverse, last,
    mixed, gated,
    ids_in, spec_out, spec_in, spec_f, ext, sig_out, sig_in, conv_out, conv_in,
    gat, wg, part, pair_out, pair_in, red_out, red_in,
    s_ids, s_spec, s_sig, s_conv, s_wy, s_wx, s_gat, s_pair, s_red,
):
    seq = lax.axis_index("seq")
    chan = lax.axis_index("chan")
    x, zl, y = seq // (NZ * NY), lax.rem(seq // NY, NZ), lax.rem(seq, NY)
    zh, co = chan // 2, lax.rem(chan, 2)

    def seq_at(px, pz, py):
        return px * (NZ * NY) + pz * NY + py

    def peer(k):
        return seq_at(
            lax.rem(x + k // (NZ * NY), NX),
            lax.rem(zl + lax.rem(k // NY, NZ), NZ),
            lax.rem(y + lax.rem(k, NY), NY),
        )

    def remote(src, dst, sems, device):
        return pltpu.make_async_remote_copy(
            src_ref=src, dst_ref=dst, send_sem=sems.at[0], recv_sem=sems.at[1],
            device_id=device, device_id_type=MESH,
        )

    other_core = {"chan": zh * 2 + 1 - co}
    other_z = {"seq": seq_at(x, 1 - zl, y)}
    own_sum = jnp.logical_and(co == zl, zh // 2 == co)

    barrier = pltpu.get_barrier_semaphore()

    def greet(k, _):
        pl.semaphore_signal(barrier, inc=1, device_id={"seq": peer(k)}, device_id_type=MESH)
        return 0

    lax.fori_loop(1, SEQ, greet, 0)
    pl.semaphore_signal(barrier, inc=1, device_id=other_core, device_id_type=MESH)
    for h in range(NH):
        @pl.when(jnp.logical_not(jnp.logical_and(own_sum, zh == h)))
        def _():
            source = {"seq": seq_at(x, co, y), "chan": h * 2 + zh // 2}
            pl.semaphore_signal(barrier, inc=1, device_id=source, device_id_type=MESH)

    for r in range(2):
        for j in range(CH // 128):
            cols = pl.ds(j * 128, 128)
            pieces = [
                spec[r, a, :, cols].astype(F32).T.reshape(128 // OWN, OWN, 128) for a in range(2)
            ]
            spec_out[pl.ds(j * (128 // OWN), 128 // OWN), pl.ds(r * 16, 16), :] = (
                jnp.concatenate(pieces, 1).astype(BF16)
            )

    pl.semaphore_wait(barrier, SEQ - 1 + 1 + NH - own_sum.astype(jnp.int32))

    ids_copy = remote(ids, ids_in, s_ids, {"seq": lax.rem(seq + 1, SEQ)})
    ids_copy.start()

    def send_all(src, dst, sems):
        def one(k, _):
            d = peer(k)
            remote(src.at[d], dst.at[seq], sems, {"seq": d}).start()
            return 0

        lax.fori_loop(1, SEQ, one, 0)

    def wait_all(src, dst, sems):
        some = pl.ds(0, SEQ - 1)
        copy = remote(src.at[some], dst.at[some], sems, other_z)
        copy.wait_recv()
        copy.wait_send()

    for k in FAR_FIRST:
        remote(
            wt, wg.at[x, y], s_wy, {"seq": seq_at(x, zl, lax.rem(y + k, NY))}
        ).start()
    send_all(spec_out, spec_in, s_spec)
    wg[pl.ds(x, 1), pl.ds(y, 1)] = wt[...][None, None]
    spec_in[pl.ds(seq, 1)] = spec_out[pl.ds(seq, 1)]

    vocab = lax.broadcasted_iota(jnp.int32, (tab.shape[0], TOK), 0)

    def one_hot(row):
        return jnp.where(vocab == row[...], 1.0, 0.0).astype(F32).T.astype(BF16)

    hot = one_hot(ids)
    for g in range(4):
        cols = pl.ds(g * CH, CH)
        ext[g, pl.ds(8, TOK), :] = jnp.dot(hot, tab[:, cols], preferred_element_type=F32)
    ids_copy.wait_recv()
    before = one_hot(ids_in)[TOK - 16 :, :]
    inside = jnp.where(seq > 0, 1.0, 0.0).astype(F32)
    for g in range(3):
        cols = pl.ds(g * CH, CH)
        halo = jnp.dot(before, tab[:, cols], preferred_element_type=F32)
        ext[g, pl.ds(0, 8), :] = halo[8:, :] * inside

    def shortened(g):
        weights = taps[g].astype(F32)
        out = weights[0:1] * ext[g, pl.ds(8, TOK), :]
        out = out + weights[1:2] * ext[g, pl.ds(7, TOK), :]
        return out + weights[2:3] * ext[g, pl.ds(6, TOK), :]

    signal = (shortened(1) * shortened(2)).astype(BF16).astype(F32)
    for j in range(CH // 128):
        block = signal[:, j * 128 : (j + 1) * 128].T
        n = 128 // OWN
        sig_out[pl.ds(j * n, n)] = block.reshape(n, OWN, TOK)
    send_all(sig_out, sig_in, s_sig)
    sig_in[pl.ds(seq, 1)] = sig_out[pl.ds(seq, 1)]

    some = pl.ds(0, NY - 1)
    wy = remote(wg.at[0, some], wg.at[0, some], s_wy, other_z)
    wy.wait_recv()
    for k in (2, 1, 3):
        remote(
            wg.at[x], wg.at[x], s_wx, {"seq": seq_at(lax.rem(x + k, NX), zl, y)}
        ).start()

    wait_all(spec_out, spec_in, s_spec)
    spec_f[...] = spec_in[...].astype(F32)
    wait_all(sig_out, sig_in, s_sig)
    cos, sin = twid[0], twid[1]
    for c in range(OWN):
        s = sig_in[:, c, :].astype(BF16)
        z = jnp.dot(first[...], jnp.concatenate([s, s], 0), preferred_element_type=F32)
        zr, zi = z[:128], z[128:]
        z = jnp.concatenate([zr * cos + zi * sin, zi * cos - zr * sin], 1).astype(BF16)
        f = jnp.dot(z, forward[...], preferred_element_type=F32)
        fr, fi = f[:, :128], f[:, 128:]
        hr = jnp.concatenate([spec_f[:, c, :], spec_f[:, 8 + c, :]], 0)
        hi = jnp.concatenate([spec_f[:, 16 + c, :], spec_f[:, 24 + c, :]], 0)
        f = jnp.concatenate([fr * hr - fi * hi, fr * hi + fi * hr], 1).astype(BF16)
        b = jnp.dot(f, inverse[...], preferred_element_type=F32)
        br, bi = b[:, :128], b[:, 128:]
        b = jnp.concatenate([br * cos - bi * sin, bi * cos + br * sin], 0).astype(BF16)
        conv_out[:, c, :] = jnp.dot(last[...], b, preferred_element_type=F32)
    send_all(conv_out, conv_in, s_conv)
    conv_in[pl.ds(seq, 1)] = conv_out[pl.ds(seq, 1)]

    query = shortened(0)
    wait_all(conv_out, conv_in, s_conv)
    for j in range(CH // 128):
        n = 128 // OWN
        block = conv_in[pl.ds(j * n, n)].reshape(128, TOK).T
        value = (query[:, j * 128 : (j + 1) * 128] * block).astype(BF16)
        gated[:, pl.ds(j * 128, 128)] = value
        gat[pl.ds(zl, 1), :, pl.ds(j * 128, 128)] = value[None]
    gat_copy = remote(gat.at[zl], gat.at[zl], s_gat, other_z)
    gat_copy.start()

    some = pl.ds(0, NX - 1)
    wx = remote(wg.at[some], wg.at[some], s_wx, other_z)
    wx.wait_recv()
    for turn in range(2):
        t = zl if turn == 0 else 1 - zl
        if turn == 1:
            gat_copy.wait_recv()
        rows = gat[t]

        def project(block):
            weights = wg[block].reshape(NY * 64, CH)
            return lax.dot_general(
                rows, weights, (((1,), (1,)), ((), ())), preferred_element_type=F32
            )

        for i in range(2):
            pair_out[turn, i] = project(2 * (1 - co) + i).astype(BF16)
        pair_copy = remote(pair_out.at[turn], pair_in.at[turn], s_pair.at[turn], other_core)
        pair_copy.start()
        for i in range(2):
            part[turn, i] = project(2 * co + i)
        pair_copy.wait_recv()
        for i in range(2):
            red_out[turn, i] = (part[turn, i] + pair_in[turn, i].astype(F32)).astype(BF16)

        for i in range(2):
            to = {"seq": seq_at(x, t, y), "chan": (2 * co + i) * 2 + zl}
            copy = remote(red_out.at[turn, i], red_in.at[zh], s_red, to)
            if turn == 1:
                copy.start()
                continue

            own = jnp.logical_and(own_sum, 2 * co + i == zh)

            @pl.when(own)
            def _():
                red_in[pl.ds(zh, 1)] = red_out[0, pl.ds(i, 1)]

            @pl.when(jnp.logical_not(own))
            def _():
                copy.start()

    for count in (NH - 1, NH):
        @pl.when(own_sum == (count == NH - 1))
        def _():
            some = pl.ds(0, count)
            copy = remote(red_in.at[some], red_in.at[some], s_red, other_z)
            copy.wait_recv()
            copy.wait_send()

    total = ext[3, pl.ds(8, TOK), :]
    for h in range(NH):
        total = total + red_in[h].astype(F32)
    mixed[...] = total.astype(BF16)

    ids_copy.wait_send()
    wy.wait_send()
    wx.wait_send()
    gat_copy.wait_send()
    for turn in range(2):
        remote(pair_out.at[turn], pair_in.at[turn], s_pair.at[turn], other_core).wait_send()


def per_device(token_ids, vocab_table, short_taps, filter_spec, out_weight):
    first, twid, forward, inverse, last = tables()
    vmem = pl.BlockSpec(memory_space=pltpu.VMEM)
    out = jax.ShapeDtypeStruct((TOK, CH), BF16)
    args = (
        token_ids.reshape(1, TOK),
        vocab_table.reshape(vocab_table.shape[0], 4 * CH),
        short_taps,
        filter_spec,
        out_weight.T,
        first, twid, forward, inverse, last,
    )
    args = tuple(jnp.asarray(arg) for arg in args)
    dma2 = pltpu.SemaphoreType.DMA((2,))
    return pl.pallas_call(
        kernel,
        out_shape=(out, out),
        in_specs=[vmem] * len(args),
        out_specs=(vmem, vmem),
        scratch_shapes=[
            pltpu.VMEM((1, TOK), jnp.int32),
            pltpu.VMEM((SEQ, 32, 128), BF16),
            pltpu.VMEM((SEQ, 32, 128), BF16),
            pltpu.VMEM((SEQ, 32, 128), F32),
            pltpu.VMEM((4, 8 + TOK, CH), F32),
            pltpu.VMEM((SEQ, OWN, TOK), F32),
            pltpu.VMEM((SEQ, OWN, TOK), F32),
            pltpu.VMEM((SEQ, OWN, TOK), F32),
            pltpu.VMEM((SEQ, OWN, TOK), F32),
            pltpu.VMEM((NZ, TOK, CH), BF16),
            pltpu.VMEM((NX, NY, 64, CH), BF16),
            pltpu.VMEM((2, 2, TOK, CH), F32),
            pltpu.VMEM((2, 2, TOK, CH), BF16),
            pltpu.VMEM((2, 2, TOK, CH), BF16),
            pltpu.VMEM((2, 2, TOK, CH), BF16),
            pltpu.VMEM((NH, TOK, CH), BF16),
            dma2, dma2, dma2, dma2, dma2, dma2, dma2,
            pltpu.SemaphoreType.DMA((2, 2)),
            dma2,
        ],
        compiler_params=pltpu.CompilerParams(
            collective_id=0, has_side_effects=True, vmem_limit_bytes=48 << 20
        ),
        name="hyena",
    )(*args)


def solution(mesh):
    placed = (
        P("seq"),
        P(None, None, "chan"),
        P(None, None, "chan"),
        P(None, "seq", None, "chan"),
        P("chan", "seq"),
    )
    return jax.shard_map(
        per_device,
        mesh=mesh,
        in_specs=placed,
        out_specs=(P("seq", "chan"), P("seq", "chan")),
        check_vma=False,
    )
```

```python
import jax
import jax.numpy as jnp
import numpy as np
from jax import lax
from jax.experimental import pallas as pl
from jax.experimental.pallas import tpu as pltpu
from jax.sharding import PartitionSpec as P

MESH = pl.DeviceIdType.MESH
F32 = jnp.float32
BF16 = jnp.bfloat16

NX, NZ, NY = 4, 2, 8
NH = 4
SEQ = NX * NZ * NY
TOK = 128
CH = 512
OWN = CH // SEQ
LEN = 2 * SEQ * TOK
NEAR_FIRST = (1, 7, 2, 6, 3, 5, 4)


def tables():
    a = np.concatenate([np.arange(0, 128, 2), np.arange(1, 128, 2)])
    p = np.arange(SEQ)
    m = np.arange(TOK)
    t1 = 2 * np.pi * (np.outer(a, p) % 128) / 128
    first = np.concatenate([np.cos(t1), -np.sin(t1)], 0)
    hi = first.astype(jnp.bfloat16)
    lo = (first - hi.astype(np.float64)).astype(jnp.bfloat16)
    first = np.concatenate([hi, lo], 1)
    tw = 2 * np.pi * (np.outer(a, m) % LEN) / LEN
    twid = np.stack([np.cos(tw), np.sin(tw)]).astype(np.float32)
    t2 = 2 * np.pi * (np.outer(m, m) % 128) / 128
    c2, s2 = np.cos(t2), np.sin(t2)
    forward = np.block([[c2, -s2], [s2, c2]]).astype(jnp.bfloat16)
    inverse = np.block([[c2, s2], [-s2, c2]]).astype(jnp.bfloat16)
    last = (np.concatenate([np.cos(t1), -np.sin(t1)], 0).T / LEN).astype(jnp.bfloat16)
    return first, twid, forward, inverse, last


def kernel(
    ids, tab, taps, spec, wt, first, twid, forward, inverse, last,
    mixed, gated,
    ids_in, spec_out, spec_in, spec_f, ext, sig_out, sig_in, conv_out, conv_in,
    gat, wy, wg, red_out, red_in,
    s_ids, s_spec, s_sig, s_conv, s_wy, s_wyr, s_wx, s_wl, s_gat, s_red,
):
    seq = lax.axis_index("seq")
    chan = lax.axis_index("chan")
    x, zl, y = seq // (NZ * NY), lax.rem(seq // NY, NZ), lax.rem(seq, NY)
    zh, co = chan // 2, lax.rem(chan, 2)

    def seq_at(px, pz, py):
        return px * (NZ * NY) + pz * NY + py

    def peer(k):
        return seq_at(
            lax.rem(x + k // (NZ * NY), NX),
            lax.rem(zl + lax.rem(k // NY, NZ), NZ),
            lax.rem(y + lax.rem(k, NY), NY),
        )

    def remote(src, dst, sems, device):
        return pltpu.make_async_remote_copy(
            src_ref=src, dst_ref=dst, send_sem=sems.at[0], recv_sem=sems.at[1],
            device_id=device, device_id_type=MESH,
        )

    other_core = {"chan": zh * 2 + 1 - co}
    other_z = {"seq": seq_at(x, 1 - zl, y)}
    own_sum = jnp.logical_and(co == zl, zh // 2 == co)

    barrier = pltpu.get_barrier_semaphore()

    def greet(k, _):
        pl.semaphore_signal(barrier, inc=1, device_id={"seq": peer(k)}, device_id_type=MESH)
        return 0

    lax.fori_loop(1, SEQ, greet, 0)
    for k in range(NX):
        beside = {"seq": seq_at(lax.rem(x + k, NX), zl, y), "chan": zh * 2 + 1 - co}
        pl.semaphore_signal(barrier, inc=1, device_id=beside, device_id_type=MESH)
    for h in range(NH):
        @pl.when(jnp.logical_not(jnp.logical_and(own_sum, zh == h)))
        def _():
            source = {"seq": seq_at(x, co, y), "chan": h * 2 + zh // 2}
            pl.semaphore_signal(barrier, inc=1, device_id=source, device_id_type=MESH)

    for r in range(2):
        for j in range(CH // 128):
            cols = pl.ds(j * 128, 128)
            pieces = [
                spec[r, a, :, cols].astype(F32).T.reshape(128 // OWN, OWN, 128) for a in range(2)
            ]
            spec_out[pl.ds(j * (128 // OWN), 128 // OWN), pl.ds(r * 16, 16), :] = (
                jnp.concatenate(pieces, 1).astype(BF16)
            )

    vocab = lax.broadcasted_iota(jnp.int32, (tab.shape[0], TOK), 0)

    def one_hot(row):
        return jnp.where(vocab == row[...], 1.0, 0.0).astype(F32).T.astype(BF16)

    hot = one_hot(ids)
    for g in range(4):
        cols = pl.ds(g * CH, CH)
        ext[g, pl.ds(8, TOK), :] = jnp.dot(hot, tab[:, cols], preferred_element_type=F32)
    pl.semaphore_wait(barrier, SEQ - 1 + NX + NH - own_sum.astype(jnp.int32))

    ids_copy = remote(ids, ids_in, s_ids, {"seq": lax.rem(seq + 1, SEQ)})
    ids_copy.start()

    def send_all(src, dst, sems):
        def one(k, _):
            d = peer(k)
            remote(src.at[d], dst.at[seq], sems, {"seq": d}).start()
            return 0

        lax.fori_loop(1, SEQ, one, 0)

    def wait_all(src, dst, sems):
        some = pl.ds(0, SEQ - 1)
        copy = remote(src.at[some], dst.at[some], sems, other_z)
        copy.wait_recv()
        copy.wait_send()

    ahead = 1 - 2 * co
    keeps = co == x // 2

    def row_of(k):
        return lax.rem(y + NY + ahead * k, NY)

    def along_y(block, way):
        return pltpu.make_async_remote_copy(
            src_ref=wy.at[block], dst_ref=wy.at[block],
            send_sem=s_wy.at[0], recv_sem=s_wyr.at[block],
            device_id={"seq": seq_at(x, zl, row_of(way))}, device_id_type=MESH,
        )

    def along_x(block):
        slot = wg.at[2 * co + lax.rem(x, 2), block]
        for k in (2, 1, 3):
            to = {"seq": seq_at(lax.rem(x + k, NX), zl, y), "chan": zh * 2 + x // 2}
            remote(wy.at[block], slot, s_wx, to).start()

        @pl.when(keeps)
        def _():
            pltpu.make_async_copy(wy.at[block], slot, s_wl).start()

        @pl.when(jnp.logical_not(keeps))
        def _():
            remote(wy.at[block], slot, s_wx, other_core).start()

    def weights_step(step):
        for way in (1, -1):
            if step > NY // 2 - (way < 0):
                continue
            along_y(row_of(-way * step), way).wait_recv()
            if step < NY // 2 - (way < 0):
                along_y(row_of(-way * step), way).start()
            along_x(row_of(-way * step))

    wy[pl.ds(y, 1)] = wt[...][None]
    along_y(y, 1).start()
    along_y(y, -1).start()
    along_x(y)
    send_all(spec_out, spec_in, s_spec)
    spec_in[pl.ds(seq, 1)] = spec_out[pl.ds(seq, 1)]
    weights_step(1)

    ids_copy.wait_recv()
    before = one_hot(ids_in)[TOK - 16 :, :]
    inside = jnp.where(seq > 0, 1.0, 0.0).astype(F32)
    for g in range(3):
        cols = pl.ds(g * CH, CH)
        halo = jnp.dot(before, tab[:, cols], preferred_element_type=F32)
        ext[g, pl.ds(0, 8), :] = halo[8:, :] * inside

    def shortened(g):
        weights = taps[g].astype(F32)
        out = weights[0:1] * ext[g, pl.ds(8, TOK), :]
        out = out + weights[1:2] * ext[g, pl.ds(7, TOK), :]
        return out + weights[2:3] * ext[g, pl.ds(6, TOK), :]

    signal = (shortened(1) * shortened(2)).astype(BF16).astype(F32)
    for j in range(CH // 128):
        block = signal[:, j * 128 : (j + 1) * 128].T
        n = 128 // OWN
        sig_out[pl.ds(j * n, n)] = block.reshape(n, OWN, TOK)
    send_all(sig_out, sig_in, s_sig)
    sig_in[pl.ds(seq, 1)] = sig_out[pl.ds(seq, 1)]

    weights_step(2)
    weights_step(3)
    wait_all(spec_out, spec_in, s_spec)
    spec_f[...] = spec_in[...].astype(F32)
    weights_step(4)
    wait_all(sig_out, sig_in, s_sig)
    cos, sin = twid[0], twid[1]
    for c in range(OWN):
        s = sig_in[:, c, :].astype(BF16)
        z = jnp.dot(first[...], jnp.concatenate([s, s], 0), preferred_element_type=F32)
        zr, zi = z[:128], z[128:]
        z = jnp.concatenate([zr * cos + zi * sin, zi * cos - zr * sin], 1).astype(BF16)
        f = jnp.dot(z, forward[...], preferred_element_type=F32)
        fr, fi = f[:, :128], f[:, 128:]
        hr = jnp.concatenate([spec_f[:, c, :], spec_f[:, 8 + c, :]], 0)
        hi = jnp.concatenate([spec_f[:, 16 + c, :], spec_f[:, 24 + c, :]], 0)
        f = jnp.concatenate([fr * hr - fi * hi, fr * hi + fi * hr], 1).astype(BF16)
        b = jnp.dot(f, inverse[...], preferred_element_type=F32)
        br, bi = b[:, :128], b[:, 128:]
        b = jnp.concatenate([br * cos - bi * sin, bi * cos + br * sin], 0).astype(BF16)
        conv_out[:, c, :] = jnp.dot(last[...], b, preferred_element_type=F32)
    send_all(conv_out, conv_in, s_conv)
    conv_in[pl.ds(seq, 1)] = conv_out[pl.ds(seq, 1)]

    query = shortened(0)
    wait_all(conv_out, conv_in, s_conv)
    for j in range(CH // 128):
        n = 128 // OWN
        block = conv_in[pl.ds(j * n, n)].reshape(128, TOK).T
        value = (query[:, j * 128 : (j + 1) * 128] * block).astype(BF16)
        gated[:, pl.ds(j * 128, 128)] = value
        gat[pl.ds(zl, 1), pl.ds(co, 1), :, pl.ds(j * 128, 128)] = value[None, None]
    own = gat.at[zl, co]
    to_core = remote(own, own, s_gat.at[0], other_core)
    to_core.start()
    to_z = remote(own, own, s_gat.at[1], other_z)
    to_z.start()

    for count in (3, 4):
        @pl.when(keeps == (count == 3))
        def _():
            some = pl.ds(0, count)
            remote(wg.at[some], wg.at[some], s_wx, other_z).wait_recv()

    @pl.when(keeps)
    def _():
        pltpu.make_async_copy(wy, wg.at[2 * co + lax.rem(x, 2)], s_wl).wait()

    to_core.wait_recv()
    for turn in range(2):
        t = zl if turn == 0 else 1 - zl
        if turn == 1:
            to_z.wait_recv()
            own = gat.at[1 - zl, co]
            on = remote(own, own, s_gat.at[2], other_core)
            on.start()
            on.wait_recv()
        for i in range(2):
            total = jnp.zeros((TOK, CH), F32)
            for c in range(2):
                total = total + lax.dot_general(
                    gat[t, c], wg[2 * c + i].reshape(NY * 64, CH), (((1,), (1,)), ((), ())),
                    preferred_element_type=F32,
                )
            red_out[turn, i] = total.astype(BF16)
            to = {"seq": seq_at(x, t, y), "chan": (2 * co + i) * 2 + zl}
            copy = remote(red_out.at[turn, i], red_in.at[zh], s_red, to)
            if turn == 1:
                copy.start()
                continue

            own_block = jnp.logical_and(own_sum, 2 * co + i == zh)

            @pl.when(own_block)
            def _():
                red_in[pl.ds(zh, 1)] = red_out[0, pl.ds(i, 1)]

            @pl.when(jnp.logical_not(own_block))
            def _():
                copy.start()

    for count in (NH - 1, NH):
        @pl.when(own_sum == (count == NH - 1))
        def _():
            some = pl.ds(0, count)
            copy = remote(red_in.at[some], red_in.at[some], s_red, other_z)
            copy.wait_recv()
            copy.wait_send()

    total = ext[3, pl.ds(8, TOK), :]
    for h in range(NH):
        total = total + red_in[h].astype(F32)
    mixed[...] = total.astype(BF16)

    ids_copy.wait_send()
    some = pl.ds(0, NY - 1)
    remote(wy.at[some], wy.at[some], s_wy, other_z).wait_send()
    for count in (3, 4):
        @pl.when(keeps == (count == 3))
        def _():
            some = pl.ds(0, count)
            remote(wg.at[some], wg.at[some], s_wx, other_z).wait_send()

    to_core.wait_send()
    to_z.wait_send()
    on.wait_send()


def per_device(token_ids, vocab_table, short_taps, filter_spec, out_weight):
    first, twid, forward, inverse, last = tables()
    vmem = pl.BlockSpec(memory_space=pltpu.VMEM)
    out = jax.ShapeDtypeStruct((TOK, CH), BF16)
    args = (
        token_ids.reshape(1, TOK),
        vocab_table.reshape(vocab_table.shape[0], 4 * CH),
        short_taps,
        filter_spec,
        out_weight.T,
        first, twid, forward, inverse, last,
    )
    args = tuple(jnp.asarray(arg) for arg in args)
    dma2 = pltpu.SemaphoreType.DMA((2,))
    return pl.pallas_call(
        kernel,
        out_shape=(out, out),
        in_specs=[vmem] * len(args),
        out_specs=(vmem, vmem),
        scratch_shapes=[
            pltpu.VMEM((1, TOK), jnp.int32),
            pltpu.VMEM((SEQ, 32, 128), BF16),
            pltpu.VMEM((SEQ, 32, 128), BF16),
            pltpu.VMEM((SEQ, 32, 128), F32),
            pltpu.VMEM((4, 8 + TOK, CH), F32),
            pltpu.VMEM((SEQ, OWN, TOK), F32),
            pltpu.VMEM((SEQ, OWN, TOK), F32),
            pltpu.VMEM((SEQ, OWN, TOK), F32),
            pltpu.VMEM((SEQ, OWN, TOK), F32),
            pltpu.VMEM((NZ, 2, TOK, CH), BF16),
            pltpu.VMEM((NY, 64, CH), BF16),
            pltpu.VMEM((4, NY, 64, CH), BF16),
            pltpu.VMEM((2, 2, TOK, CH), BF16),
            pltpu.VMEM((NH, TOK, CH), BF16),
            dma2, dma2, dma2, dma2, dma2,
            pltpu.SemaphoreType.DMA((NY,)),
            dma2,
            pltpu.SemaphoreType.DMA,
            pltpu.SemaphoreType.DMA((3, 2)),
            dma2,
        ],
        compiler_params=pltpu.CompilerParams(
            collective_id=0, has_side_effects=True, vmem_limit_bytes=48 << 20
        ),
        name="hyena",
    )(*args)


def solution(mesh):
    placed = (
        P("seq"),
        P(None, None, "chan"),
        P(None, None, "chan"),
        P(None, "seq", None, "chan"),
        P("chan", "seq"),
    )
    return jax.shard_map(
        per_device,
        mesh=mesh,
        in_specs=placed,
        out_specs=(P("seq", "chan"), P("seq", "chan")),
        check_vma=False,
    )
```

```python
import jax
import jax.numpy as jnp
import numpy as np
from jax import lax
from jax.experimental import pallas as pl
from jax.experimental.pallas import tpu as pltpu
from jax.sharding import PartitionSpec as P

MESH = pl.DeviceIdType.MESH
F32 = jnp.float32
BF16 = jnp.bfloat16

NX, NZ, NY = 4, 2, 8
NH = 4
SEQ = NX * NZ * NY
TOK = 128
CH = 512
GROUPS = SEQ // NZ
OWN = CH // GROUPS
LEN = 2 * SEQ * TOK
NEAR_FIRST = (1, 7, 2, 6, 3, 5, 4)


def tables():
    a = np.concatenate([np.arange(0, 128, 2), np.arange(1, 128, 2)])
    p = np.arange(SEQ)
    m = np.arange(TOK)
    t1 = 2 * np.pi * (np.outer(a, p) % 128) / 128
    first = np.concatenate([np.cos(t1), -np.sin(t1)], 0)
    hi = first.astype(jnp.bfloat16)
    lo = (first - hi.astype(np.float64)).astype(jnp.bfloat16)
    first = np.concatenate([hi, lo], 1)
    tw = 2 * np.pi * (np.outer(a, m) % LEN) / LEN
    twid = np.stack([np.cos(tw), np.sin(tw)]).astype(np.float32)
    t2 = 2 * np.pi * (np.outer(m, m) % 128) / 128
    c2, s2 = np.cos(t2), np.sin(t2)
    forward = np.block([[c2, -s2], [s2, c2]]).astype(jnp.bfloat16)
    inverse = np.block([[c2, s2], [-s2, c2]]).astype(jnp.bfloat16)
    last = (np.concatenate([np.cos(t1), -np.sin(t1)], 0).T / LEN).astype(jnp.bfloat16)
    return first, twid, forward, inverse, last


def kernel(
    ids, tab, taps, spec, wt, first, twid, forward, inverse, last,
    mixed, gated,
    ids_in, spec_out, spec_in, spec_f, spec_c, ext, sig_out, sig_in, sig_f,
    conv_f, conv_out, conv_in, query,
    gat, wy, wg, red_out, red_in,
    s_ids, s_spec, s_sig, s_query, s_conv, s_wy, s_wyr, s_wx, s_wl, s_gat, s_red,
):
    seq = lax.axis_index("seq")
    chan = lax.axis_index("chan")
    x, zl, y = seq // (NZ * NY), lax.rem(seq // NY, NZ), lax.rem(seq, NY)
    zh, co = chan // 2, lax.rem(chan, 2)

    def seq_at(px, pz, py):
        return px * (NZ * NY) + pz * NY + py

    def peer(k):
        return lax.rem(seq + k, SEQ)

    def remote(src, dst, sems, device):
        return pltpu.make_async_remote_copy(
            src_ref=src, dst_ref=dst, send_sem=sems.at[0], recv_sem=sems.at[1],
            device_id=device, device_id_type=MESH,
        )

    other_core = {"chan": zh * 2 + 1 - co}
    other_z = {"seq": seq_at(x, 1 - zl, y)}
    own_sum = jnp.logical_and(co == zl, zh // 2 == co)

    barrier = pltpu.get_barrier_semaphore()

    def greet(k, _):
        pl.semaphore_signal(barrier, inc=1, device_id={"seq": peer(k)}, device_id_type=MESH)
        return 0

    lax.fori_loop(1, SEQ, greet, 0)
    for k in range(NX):
        beside = {"seq": seq_at(lax.rem(x + k, NX), zl, y), "chan": zh * 2 + 1 - co}
        pl.semaphore_signal(barrier, inc=1, device_id=beside, device_id_type=MESH)
    for h in range(NH):
        @pl.when(jnp.logical_not(jnp.logical_and(own_sum, zh == h)))
        def _():
            source = {"seq": seq_at(x, co, y), "chan": h * 2 + zh // 2}
            pl.semaphore_signal(barrier, inc=1, device_id=source, device_id_type=MESH)

    for r in range(2):
        for j in range(CH // 128):
            cols = pl.ds(j * 128, 128)
            pieces = [
                spec[r, a, :, cols].astype(F32).T.reshape(128 // OWN, OWN, 128) for a in range(2)
            ]
            for a in range(2):
                spec_out[pl.ds(j * (128 // OWN), 128 // OWN), pl.ds((2 * r + a) * OWN, OWN), :] = (
                    pieces[a].astype(BF16)
                )

    vocab = lax.broadcasted_iota(jnp.int32, (tab.shape[0], TOK), 0)

    def one_hot(row):
        return jnp.where(vocab == row[...], 1.0, 0.0).astype(F32).T.astype(BF16)

    hot = one_hot(ids)
    for g in range(4):
        cols = pl.ds(g * CH, CH)
        ext[g, pl.ds(8, TOK), :] = jnp.dot(hot, tab[:, cols], preferred_element_type=F32)
    pl.semaphore_wait(barrier, SEQ - 1 + NX + NH - own_sum.astype(jnp.int32))

    ids_copy = remote(ids, ids_in, s_ids, {"seq": lax.rem(seq + 1, SEQ)})
    ids_copy.start()

    active = zl == co
    group = x * NY + y

    def send_groups(src, dst, sems):
        def one(k, _):
            u = lax.rem(group + k, GROUPS)
            to = {"seq": seq_at(u // NY, co, lax.rem(u, NY))}
            remote(src.at[u], dst.at[seq], sems, to).start()
            return 0

        lax.fori_loop(1, GROUPS, one, 0)

        @pl.when(active)
        def _():
            dst[pl.ds(seq, 1)] = src[pl.ds(group, 1)]

        @pl.when(jnp.logical_not(active))
        def _():
            remote(src.at[group], dst.at[seq], sems, other_z).start()

    def wait_blocks(ref, count, sems, sent):
        some = pl.ds(0, count)
        copy = remote(ref.at[some], ref.at[some], sems, other_z)
        if sent:
            copy.wait_send()
        else:
            copy.wait_recv()

    ahead = 1 - 2 * co
    keeps = co == x // 2

    def row_of(k):
        return lax.rem(y + NY + ahead * k, NY)

    def along_y(block, way):
        return pltpu.make_async_remote_copy(
            src_ref=wy.at[block], dst_ref=wy.at[block],
            send_sem=s_wy.at[0], recv_sem=s_wyr.at[block],
            device_id={"seq": seq_at(x, zl, row_of(way))}, device_id_type=MESH,
        )

    def along_x(block):
        slot = wg.at[2 * co + lax.rem(x, 2), block]
        for k in (2, 1, 3):
            to = {"seq": seq_at(lax.rem(x + k, NX), zl, y), "chan": zh * 2 + x // 2}
            remote(wy.at[block], slot, s_wx, to).start()

        @pl.when(keeps)
        def _():
            pltpu.make_async_copy(wy.at[block], slot, s_wl).start()

        @pl.when(jnp.logical_not(keeps))
        def _():
            remote(wy.at[block], slot, s_wx, other_core).start()

    def weights_step(step):
        for way in (1, -1):
            if step > NY // 2 - (way < 0):
                continue
            along_y(row_of(-way * step), way).wait_recv()
            if step < NY // 2 - (way < 0):
                along_y(row_of(-way * step), way).start()
            along_x(row_of(-way * step))

    wy[pl.ds(y, 1)] = wt[...][None]
    along_y(y, 1).start()
    along_y(y, -1).start()
    along_x(y)
    send_groups(spec_out, spec_in, s_spec)
    weights_step(1)

    ids_copy.wait_recv()
    before = one_hot(ids_in)[TOK - 16 :, :]
    inside = jnp.where(seq > 0, 1.0, 0.0).astype(F32)
    for g in range(3):
        cols = pl.ds(g * CH, CH)
        halo = jnp.dot(before, tab[:, cols], preferred_element_type=F32)
        ext[g, pl.ds(0, 8), :] = halo[8:, :] * inside

    def shortened(g):
        weights = taps[g].astype(F32)
        out = weights[0:1] * ext[g, pl.ds(8, TOK), :]
        out = out + weights[1:2] * ext[g, pl.ds(7, TOK), :]
        return out + weights[2:3] * ext[g, pl.ds(6, TOK), :]

    signal = shortened(1) * shortened(2)
    for j in range(CH // 128):
        block = signal[:, j * 128 : (j + 1) * 128].T
        n = 128 // OWN
        sig_out[pl.ds(j * n, n)] = block.reshape(n, OWN, TOK).astype(BF16)
    send_groups(sig_out, sig_in, s_sig)
    query[pl.ds(zl, 1)] = shortened(0)[None]
    query_copy = remote(query.at[zl], query.at[zl], s_query, other_z)
    query_copy.start()

    weights_step(2)
    weights_step(3)

    @pl.when(active)
    def _():
        wait_blocks(spec_in, SEQ - 1, s_spec, False)
        spec_f[...] = spec_in[...].astype(F32)
        for c in range(OWN):
            for n in range(4):
                spec_c[c, n] = spec_f[:, OWN * n + c, :]

    weights_step(4)

    @pl.when(active)
    def _():
        wait_blocks(sig_in, SEQ - 1, s_sig, False)
        sig_f[...] = sig_in[...].astype(F32)
        cos, sin = twid[0], twid[1]
        for start in range(0, OWN, 4):
            some = range(start, start + 4)
            lines = jnp.concatenate([sig_f[:, c, :] for c in some], 1).astype(BF16)
            lines = jnp.concatenate([lines, lines], 0)
            z_all = jnp.dot(first[...], lines, preferred_element_type=F32)
            zs = []
            for n in range(4):
                zr, zi = z_all[:128, n * 128 : n * 128 + 128], z_all[128:, n * 128 : n * 128 + 128]
                z = jnp.concatenate([zr * cos + zi * sin, zi * cos - zr * sin], 1)
                zs.append(z.astype(BF16))
            f_all = jnp.dot(jnp.concatenate(zs, 0), forward[...], preferred_element_type=F32)
            fs = []
            for n, c in enumerate(some):
                fr, fi = f_all[n * 128 : n * 128 + 128, :128], f_all[n * 128 : n * 128 + 128, 128:]
                hr = spec_c[c, :2].reshape(128, 128)
                hi = spec_c[c, 2:].reshape(128, 128)
                fs.append(jnp.concatenate([fr * hr - fi * hi, fr * hi + fi * hr], 1).astype(BF16))
            b_all = jnp.dot(jnp.concatenate(fs, 0), inverse[...], preferred_element_type=F32)
            bs = []
            for n in range(4):
                br, bi = b_all[n * 128 : n * 128 + 128, :128], b_all[n * 128 : n * 128 + 128, 128:]
                b = jnp.concatenate([br * cos - bi * sin, bi * cos + br * sin], 0)
                bs.append(b.astype(BF16))
            out = jnp.dot(last[...], jnp.concatenate(bs, 1), preferred_element_type=F32)
            for n, c in enumerate(some):
                conv_f[:, c, :] = out[:, n * 128 : n * 128 + 128]
        conv_out[...] = conv_f[...].astype(BF16)

        def flip(d):
            return d + NY * (1 - 2 * lax.rem(d // NY, NZ))

        for turn in range(2):
            def back(k, _):
                d = lax.rem(seq + k, SEQ)
                block = flip(d) if turn else d
                remote(
                    conv_out.at[block], conv_in.at[turn, group], s_conv.at[turn], {"seq": d}
                ).start()
                return 0

            lax.fori_loop(1, SEQ, back, 0)
            block = flip(seq) if turn else seq
            conv_in[turn, pl.ds(group, 1)] = conv_out[pl.ds(block, 1)]

    def gate(turn):
        for count in (GROUPS - 1, GROUPS):
            @pl.when(active == (count == GROUPS - 1))
            def _():
                wait_blocks(conv_in.at[turn], count, s_conv.at[turn], False)

        t = 1 - zl if turn else zl
        if turn:
            query_copy.wait_recv()
        for j in range(CH // 128):
            n = 128 // OWN
            cols = pl.ds(j * 128, 128)
            block = conv_in[turn, pl.ds(j * n, n)].astype(F32).reshape(128, TOK).T
            value = (query[t, :, cols] * block).astype(BF16)
            if turn == 0:
                gated[:, cols] = value
            gat[turn, pl.ds(co, 1), :, cols] = value[None]
        own = gat.at[turn, co]
        to_core = remote(own, own, s_gat.at[turn], other_core)
        to_core.start()
        return to_core

    to_cores = [gate(0)]

    for count in (3, 4):
        @pl.when(keeps == (count == 3))
        def _():
            some = pl.ds(0, count)
            remote(wg.at[some], wg.at[some], s_wx, other_z).wait_recv()

    @pl.when(keeps)
    def _():
        pltpu.make_async_copy(wy, wg.at[2 * co + lax.rem(x, 2)], s_wl).wait()

    for turn in range(2):
        t = zl if turn == 0 else 1 - zl
        if turn == 1:
            to_cores.append(gate(1))
        to_cores[turn].wait_recv()
        for i in range(2):
            total = jnp.zeros((TOK, CH), F32)
            for c in range(2):
                total = total + lax.dot_general(
                    gat[turn, c], wg[2 * c + i].reshape(NY * 64, CH), (((1,), (1,)), ((), ())),
                    preferred_element_type=F32,
                )
            red_out[turn, i] = total.astype(BF16)
            to = {"seq": seq_at(x, t, y), "chan": (2 * co + i) * 2 + zl}
            copy = remote(red_out.at[turn, i], red_in.at[zh], s_red, to)
            if turn == 1:
                copy.start()
                continue

            own_block = jnp.logical_and(own_sum, 2 * co + i == zh)

            @pl.when(own_block)
            def _():
                red_in[pl.ds(zh, 1)] = red_out[0, pl.ds(i, 1)]

            @pl.when(jnp.logical_not(own_block))
            def _():
                copy.start()

    for count in (NH - 1, NH):
        @pl.when(own_sum == (count == NH - 1))
        def _():
            some = pl.ds(0, count)
            copy = remote(red_in.at[some], red_in.at[some], s_red, other_z)
            copy.wait_recv()
            copy.wait_send()

    total = ext[3, pl.ds(8, TOK), :]
    for h in range(NH):
        total = total + red_in[h].astype(F32)
    mixed[...] = total.astype(BF16)

    ids_copy.wait_send()
    for count in (GROUPS - 1, GROUPS):
        @pl.when(active == (count == GROUPS - 1))
        def _():
            wait_blocks(spec_out, count, s_spec, True)
            wait_blocks(sig_out, count, s_sig, True)

    @pl.when(active)
    def _():
        for turn in range(2):
            wait_blocks(conv_out, SEQ - 1, s_conv.at[turn], True)

    some = pl.ds(0, NY - 1)
    remote(wy.at[some], wy.at[some], s_wy, other_z).wait_send()
    for count in (3, 4):
        @pl.when(keeps == (count == 3))
        def _():
            some = pl.ds(0, count)
            remote(wg.at[some], wg.at[some], s_wx, other_z).wait_send()

    query_copy.wait_send()
    for copy in to_cores:
        copy.wait_send()


def per_device(token_ids, vocab_table, short_taps, filter_spec, out_weight):
    first, twid, forward, inverse, last = tables()
    vmem = pl.BlockSpec(memory_space=pltpu.VMEM)
    out = jax.ShapeDtypeStruct((TOK, CH), BF16)
    args = (
        token_ids.reshape(1, TOK),
        vocab_table.reshape(vocab_table.shape[0], 4 * CH),
        short_taps,
        filter_spec,
        out_weight.T,
        first, twid, forward, inverse, last,
    )
    args = tuple(jnp.asarray(arg) for arg in args)
    dma2 = pltpu.SemaphoreType.DMA((2,))
    return pl.pallas_call(
        kernel,
        out_shape=(out, out),
        in_specs=[vmem] * len(args),
        out_specs=(vmem, vmem),
        scratch_shapes=[
            pltpu.VMEM((1, TOK), jnp.int32),
            pltpu.VMEM((GROUPS, 4 * OWN, 128), BF16),
            pltpu.VMEM((SEQ, 4 * OWN, 128), BF16),
            pltpu.VMEM((SEQ, 4 * OWN, 128), F32),
            pltpu.VMEM((OWN, 4, SEQ, 128), F32),
            pltpu.VMEM((4, 8 + TOK, CH), F32),
            pltpu.VMEM((GROUPS, OWN, TOK), BF16),
            pltpu.VMEM((SEQ, OWN, TOK), BF16),
            pltpu.VMEM((SEQ, OWN, TOK), F32),
            pltpu.VMEM((SEQ, OWN, TOK), F32),
            pltpu.VMEM((SEQ, OWN, TOK), BF16),
            pltpu.VMEM((2, GROUPS, OWN, TOK), BF16),
            pltpu.VMEM((NZ, TOK, CH), F32),
            pltpu.VMEM((NZ, 2, TOK, CH), BF16),
            pltpu.VMEM((NY, 64, CH), BF16),
            pltpu.VMEM((4, NY, 64, CH), BF16),
            pltpu.VMEM((2, 2, TOK, CH), BF16),
            pltpu.VMEM((NH, TOK, CH), BF16),
            dma2, dma2, dma2, dma2,
            pltpu.SemaphoreType.DMA((2, 2)),
            dma2,
            pltpu.SemaphoreType.DMA((NY,)),
            dma2,
            pltpu.SemaphoreType.DMA,
            pltpu.SemaphoreType.DMA((2, 2)),
            dma2,
        ],
        compiler_params=pltpu.CompilerParams(
            collective_id=0, has_side_effects=True, vmem_limit_bytes=48 << 20
        ),
        name="hyena",
    )(*args)


def solution(mesh):
    placed = (
        P("seq"),
        P(None, None, "chan"),
        P(None, None, "chan"),
        P(None, "seq", None, "chan"),
        P("chan", "seq"),
    )
    return jax.shard_map(
        per_device,
        mesh=mesh,
        in_specs=placed,
        out_specs=(P("seq", "chan"), P("seq", "chan")),
        check_vma=False,
    )
```

```python
import jax
import jax.numpy as jnp
import numpy as np
from jax import lax
from jax.experimental import pallas as pl
from jax.experimental.pallas import tpu as pltpu
from jax.sharding import PartitionSpec as P

MESH = pl.DeviceIdType.MESH
F32 = jnp.float32
BF16 = jnp.bfloat16

NX, NZ, NY = 4, 2, 8
NH = 4
SEQ = NX * NZ * NY
TOK = 128
CH = 512
GROUPS = SEQ // NZ
OWN = CH // GROUPS
LEN = 2 * SEQ * TOK
NEAR_FIRST = (1, 7, 2, 6, 3, 5, 4)


def tables():
    a = np.concatenate([np.arange(0, 128, 2), np.arange(1, 128, 2)])
    p = np.arange(SEQ)
    m = np.arange(TOK)
    t1 = 2 * np.pi * (np.outer(a, p) % 128) / 128
    first = np.concatenate([np.cos(t1), -np.sin(t1)], 0)
    hi = first.astype(jnp.bfloat16)
    lo = (first - hi.astype(np.float64)).astype(jnp.bfloat16)
    first = np.concatenate([hi, lo], 1)
    tw = 2 * np.pi * (np.outer(a, m) % LEN) / LEN
    twid = np.stack([np.cos(tw), np.sin(tw)]).astype(np.float32)
    t2 = 2 * np.pi * (np.outer(m, m) % 128) / 128
    c2, s2 = np.cos(t2), np.sin(t2)
    forward = np.block([[c2, -s2], [s2, c2]]).astype(jnp.bfloat16)
    inverse = np.block([[c2, s2], [-s2, c2]]).astype(jnp.bfloat16)
    last = (np.concatenate([np.cos(t1), -np.sin(t1)], 0).T / LEN).astype(jnp.bfloat16)
    return first, twid, forward, inverse, last


def each(start, stop, one, width=8):
    steps = (stop - start) // width

    def some(n, _):
        for i in range(width):
            one(start + n * width + i)
        return 0

    lax.fori_loop(0, steps, some, 0)
    for k in range(start + steps * width, stop):
        one(k)


def kernel(
    ids, tab, taps, spec, wt, first, twid, forward, inverse, last,
    mixed, gated,
    ids_in, spec_out, spec_in, spec_f, spec_c, ext, sig_out, sig_in, sig_f,
    conv_f, conv_out, conv_in, query,
    gat, wy, wg, red_out, red_in,
    s_ids, s_spec, s_sig, s_query, s_conv, s_wy, s_wyr, s_wx, s_wl, s_gat, s_red,
):
    seq = lax.axis_index("seq")
    chan = lax.axis_index("chan")
    x, zl, y = seq // (NZ * NY), lax.rem(seq // NY, NZ), lax.rem(seq, NY)
    zh, co = chan // 2, lax.rem(chan, 2)

    def seq_at(px, pz, py):
        return px * (NZ * NY) + pz * NY + py

    def peer(k):
        return lax.rem(seq + k, SEQ)

    def remote(src, dst, sems, device):
        return pltpu.make_async_remote_copy(
            src_ref=src, dst_ref=dst, send_sem=sems.at[0], recv_sem=sems.at[1],
            device_id=device, device_id_type=MESH,
        )

    other_core = {"chan": zh * 2 + 1 - co}
    other_z = {"seq": seq_at(x, 1 - zl, y)}
    own_sum = jnp.logical_and(co == zl, zh // 2 == co)

    barrier = pltpu.get_barrier_semaphore()

    def greet(k):
        pl.semaphore_signal(barrier, inc=1, device_id={"seq": peer(k)}, device_id_type=MESH)

    each(1, SEQ, greet)
    for k in range(NX):
        beside = {"seq": seq_at(lax.rem(x + k, NX), zl, y), "chan": zh * 2 + 1 - co}
        pl.semaphore_signal(barrier, inc=1, device_id=beside, device_id_type=MESH)
    for h in range(NH):
        @pl.when(jnp.logical_not(jnp.logical_and(own_sum, zh == h)))
        def _():
            source = {"seq": seq_at(x, co, y), "chan": h * 2 + zh // 2}
            pl.semaphore_signal(barrier, inc=1, device_id=source, device_id_type=MESH)

    for r in range(2):
        for j in range(CH // 128):
            cols = pl.ds(j * 128, 128)
            pieces = [
                spec[r, a, :, cols].astype(F32).T.reshape(128 // OWN, OWN, 128) for a in range(2)
            ]
            for a in range(2):
                spec_out[pl.ds(j * (128 // OWN), 128 // OWN), pl.ds((2 * r + a) * OWN, OWN), :] = (
                    pieces[a].astype(BF16)
                )

    vocab = lax.broadcasted_iota(jnp.int32, (tab.shape[0], TOK), 0)

    def one_hot(row):
        return jnp.where(vocab == row[...], 1.0, 0.0).astype(F32).T.astype(BF16)

    hot = one_hot(ids)
    for g in range(4):
        cols = pl.ds(g * CH, CH)
        ext[g, pl.ds(8, TOK), :] = jnp.dot(hot, tab[:, cols], preferred_element_type=F32)
    pl.semaphore_wait(barrier, SEQ - 1 + NX + NH - own_sum.astype(jnp.int32))

    ids_copy = remote(ids, ids_in, s_ids, {"seq": lax.rem(seq + 1, SEQ)})
    ids_copy.start()

    active = zl == co
    group = x * NY + y

    def send_groups(src, dst, sems):
        def one(k):
            u = lax.rem(group + k, GROUPS)
            to = {"seq": seq_at(u // NY, co, lax.rem(u, NY))}
            remote(src.at[u], dst.at[seq], sems, to).start()

        each(1, GROUPS, one)

        @pl.when(active)
        def _():
            dst[pl.ds(seq, 1)] = src[pl.ds(group, 1)]

        @pl.when(jnp.logical_not(active))
        def _():
            remote(src.at[group], dst.at[seq], sems, other_z).start()

    def wait_blocks(ref, count, sems, sent):
        some = pl.ds(0, count)
        copy = remote(ref.at[some], ref.at[some], sems, other_z)
        if sent:
            copy.wait_send()
        else:
            copy.wait_recv()

    ahead = 1 - 2 * co
    keeps = co == x // 2

    def row_of(k):
        return lax.rem(y + NY + ahead * k, NY)

    def along_y(block, way):
        return pltpu.make_async_remote_copy(
            src_ref=wy.at[block], dst_ref=wy.at[block],
            send_sem=s_wy.at[0], recv_sem=s_wyr.at[block],
            device_id={"seq": seq_at(x, zl, row_of(way))}, device_id_type=MESH,
        )

    def along_x(block):
        slot = wg.at[2 * co + lax.rem(x, 2), block]
        for k in (2, 1, 3):
            to = {"seq": seq_at(lax.rem(x + k, NX), zl, y), "chan": zh * 2 + x // 2}
            remote(wy.at[block], slot, s_wx, to).start()

        @pl.when(keeps)
        def _():
            pltpu.make_async_copy(wy.at[block], slot, s_wl).start()

        @pl.when(jnp.logical_not(keeps))
        def _():
            remote(wy.at[block], slot, s_wx, other_core).start()

    def weights_step(step):
        for way in (1, -1):
            if step > NY // 2 - (way < 0):
                continue
            along_y(row_of(-way * step), way).wait_recv()
            if step < NY // 2 - (way < 0):
                along_y(row_of(-way * step), way).start()
            along_x(row_of(-way * step))

    wy[pl.ds(y, 1)] = wt[...][None]
    along_y(y, 1).start()
    along_y(y, -1).start()
    along_x(y)
    send_groups(spec_out, spec_in, s_spec)
    weights_step(1)

    ids_copy.wait_recv()
    before = one_hot(ids_in)[TOK - 16 :, :]
    inside = jnp.where(seq > 0, 1.0, 0.0).astype(F32)
    for g in range(3):
        cols = pl.ds(g * CH, CH)
        halo = jnp.dot(before, tab[:, cols], preferred_element_type=F32)
        ext[g, pl.ds(0, 8), :] = halo[8:, :] * inside

    def shortened(g):
        weights = taps[g].astype(F32)
        out = weights[0:1] * ext[g, pl.ds(8, TOK), :]
        out = out + weights[1:2] * ext[g, pl.ds(7, TOK), :]
        return out + weights[2:3] * ext[g, pl.ds(6, TOK), :]

    signal = shortened(1) * shortened(2)
    for j in range(CH // 128):
        block = signal[:, j * 128 : (j + 1) * 128].T
        n = 128 // OWN
        sig_out[pl.ds(j * n, n)] = block.reshape(n, OWN, TOK).astype(BF16)
    send_groups(sig_out, sig_in, s_sig)
    query[pl.ds(zl, 1)] = shortened(0)[None]
    query_copy = remote(query.at[zl], query.at[zl], s_query, other_z)
    query_copy.start()

    weights_step(2)
    weights_step(3)

    @pl.when(active)
    def _():
        wait_blocks(spec_in, SEQ - 1, s_spec, False)
        spec_f[...] = spec_in[...].astype(F32)
        for c in range(OWN):
            for n in range(4):
                spec_c[c, n] = spec_f[:, OWN * n + c, :]

    weights_step(4)

    @pl.when(active)
    def _():
        wait_blocks(sig_in, SEQ - 1, s_sig, False)
        sig_f[...] = sig_in[...].astype(F32)
        cos, sin = twid[0], twid[1]
        for start in range(0, OWN, 4):
            some = range(start, start + 4)
            lines = jnp.concatenate([sig_f[:, c, :] for c in some], 1).astype(BF16)
            lines = jnp.concatenate([lines, lines], 0)
            z_all = jnp.dot(first[...], lines, preferred_element_type=F32)
            zs = []
            for n in range(4):
                zr, zi = z_all[:128, n * 128 : n * 128 + 128], z_all[128:, n * 128 : n * 128 + 128]
                z = jnp.concatenate([zr * cos + zi * sin, zi * cos - zr * sin], 1)
                zs.append(z.astype(BF16))
            f_all = jnp.dot(jnp.concatenate(zs, 0), forward[...], preferred_element_type=F32)
            fs = []
            for n, c in enumerate(some):
                fr, fi = f_all[n * 128 : n * 128 + 128, :128], f_all[n * 128 : n * 128 + 128, 128:]
                hr = spec_c[c, :2].reshape(128, 128)
                hi = spec_c[c, 2:].reshape(128, 128)
                fs.append(jnp.concatenate([fr * hr - fi * hi, fr * hi + fi * hr], 1).astype(BF16))
            b_all = jnp.dot(jnp.concatenate(fs, 0), inverse[...], preferred_element_type=F32)
            bs = []
            for n in range(4):
                br, bi = b_all[n * 128 : n * 128 + 128, :128], b_all[n * 128 : n * 128 + 128, 128:]
                b = jnp.concatenate([br * cos - bi * sin, bi * cos + br * sin], 0)
                bs.append(b.astype(BF16))
            out = jnp.dot(last[...], jnp.concatenate(bs, 1), preferred_element_type=F32)
            for n, c in enumerate(some):
                conv_f[:, c, :] = out[:, n * 128 : n * 128 + 128]
        conv_out[...] = conv_f[...].astype(BF16)

        def flip(d):
            return d + NY * (1 - 2 * lax.rem(d // NY, NZ))

        for turn in range(2):
            def back(k):
                d = lax.rem(seq + k, SEQ)
                block = flip(d) if turn else d
                remote(
                    conv_out.at[block], conv_in.at[turn, group], s_conv.at[turn], {"seq": d}
                ).start()

            each(1, SEQ, back)
            block = flip(seq) if turn else seq
            conv_in[turn, pl.ds(group, 1)] = conv_out[pl.ds(block, 1)]

    def gate(turn):
        for count in (GROUPS - 1, GROUPS):
            @pl.when(active == (count == GROUPS - 1))
            def _():
                wait_blocks(conv_in.at[turn], count, s_conv.at[turn], False)

        t = 1 - zl if turn else zl
        if turn:
            query_copy.wait_recv()
        for j in range(CH // 128):
            n = 128 // OWN
            cols = pl.ds(j * 128, 128)
            block = conv_in[turn, pl.ds(j * n, n)].astype(F32).reshape(128, TOK).T
            value = (query[t, :, cols] * block).astype(BF16)
            if turn == 0:
                gated[:, cols] = value
            gat[turn, pl.ds(co, 1), :, cols] = value[None]
        own = gat.at[turn, co]
        to_core = remote(own, own, s_gat.at[turn], other_core)
        to_core.start()
        return to_core

    to_cores = [gate(0)]

    for count in (3, 4):
        @pl.when(keeps == (count == 3))
        def _():
            some = pl.ds(0, count)
            remote(wg.at[some], wg.at[some], s_wx, other_z).wait_recv()

    @pl.when(keeps)
    def _():
        pltpu.make_async_copy(wy, wg.at[2 * co + lax.rem(x, 2)], s_wl).wait()

    for turn in range(2):
        t = zl if turn == 0 else 1 - zl
        if turn == 1:
            to_cores.append(gate(1))
        to_cores[turn].wait_recv()
        for i in range(2):
            total = jnp.zeros((TOK, CH), F32)
            for c in range(2):
                total = total + lax.dot_general(
                    gat[turn, c], wg[2 * c + i].reshape(NY * 64, CH), (((1,), (1,)), ((), ())),
                    preferred_element_type=F32,
                )
            red_out[turn, i] = total.astype(BF16)
            to = {"seq": seq_at(x, t, y), "chan": (2 * co + i) * 2 + zl}
            copy = remote(red_out.at[turn, i], red_in.at[zh], s_red, to)
            if turn == 1:
                copy.start()
                continue

            own_block = jnp.logical_and(own_sum, 2 * co + i == zh)

            @pl.when(own_block)
            def _():
                red_in[pl.ds(zh, 1)] = red_out[0, pl.ds(i, 1)]

            @pl.when(jnp.logical_not(own_block))
            def _():
                copy.start()

    for count in (NH - 1, NH):
        @pl.when(own_sum == (count == NH - 1))
        def _():
            some = pl.ds(0, count)
            copy = remote(red_in.at[some], red_in.at[some], s_red, other_z)
            copy.wait_recv()
            copy.wait_send()

    total = ext[3, pl.ds(8, TOK), :]
    for h in range(NH):
        total = total + red_in[h].astype(F32)
    mixed[...] = total.astype(BF16)

    ids_copy.wait_send()
    for count in (GROUPS - 1, GROUPS):
        @pl.when(active == (count == GROUPS - 1))
        def _():
            wait_blocks(spec_out, count, s_spec, True)
            wait_blocks(sig_out, count, s_sig, True)

    @pl.when(active)
    def _():
        for turn in range(2):
            wait_blocks(conv_out, SEQ - 1, s_conv.at[turn], True)

    some = pl.ds(0, NY - 1)
    remote(wy.at[some], wy.at[some], s_wy, other_z).wait_send()
    for count in (3, 4):
        @pl.when(keeps == (count == 3))
        def _():
            some = pl.ds(0, count)
            remote(wg.at[some], wg.at[some], s_wx, other_z).wait_send()

    query_copy.wait_send()
    for copy in to_cores:
        copy.wait_send()


def per_device(token_ids, vocab_table, short_taps, filter_spec, out_weight):
    first, twid, forward, inverse, last = tables()
    vmem = pl.BlockSpec(memory_space=pltpu.VMEM)
    out = jax.ShapeDtypeStruct((TOK, CH), BF16)
    args = (
        token_ids.reshape(1, TOK),
        vocab_table.reshape(vocab_table.shape[0], 4 * CH),
        short_taps,
        filter_spec,
        out_weight.T,
        first, twid, forward, inverse, last,
    )
    args = tuple(jnp.asarray(arg) for arg in args)
    dma2 = pltpu.SemaphoreType.DMA((2,))
    return pl.pallas_call(
        kernel,
        out_shape=(out, out),
        in_specs=[vmem] * len(args),
        out_specs=(vmem, vmem),
        scratch_shapes=[
            pltpu.VMEM((1, TOK), jnp.int32),
            pltpu.VMEM((GROUPS, 4 * OWN, 128), BF16),
            pltpu.VMEM((SEQ, 4 * OWN, 128), BF16),
            pltpu.VMEM((SEQ, 4 * OWN, 128), F32),
            pltpu.VMEM((OWN, 4, SEQ, 128), F32),
            pltpu.VMEM((4, 8 + TOK, CH), F32),
            pltpu.VMEM((GROUPS, OWN, TOK), BF16),
            pltpu.VMEM((SEQ, OWN, TOK), BF16),
            pltpu.VMEM((SEQ, OWN, TOK), F32),
            pltpu.VMEM((SEQ, OWN, TOK), F32),
            pltpu.VMEM((SEQ, OWN, TOK), BF16),
            pltpu.VMEM((2, GROUPS, OWN, TOK), BF16),
            pltpu.VMEM((NZ, TOK, CH), F32),
            pltpu.VMEM((NZ, 2, TOK, CH), BF16),
            pltpu.VMEM((NY, 64, CH), BF16),
            pltpu.VMEM((4, NY, 64, CH), BF16),
            pltpu.VMEM((2, 2, TOK, CH), BF16),
            pltpu.VMEM((NH, TOK, CH), BF16),
            dma2, dma2, dma2, dma2,
            pltpu.SemaphoreType.DMA((2, 2)),
            dma2,
            pltpu.SemaphoreType.DMA((NY,)),
            dma2,
            pltpu.SemaphoreType.DMA,
            pltpu.SemaphoreType.DMA((2, 2)),
            dma2,
        ],
        compiler_params=pltpu.CompilerParams(
            collective_id=0, has_side_effects=True, vmem_limit_bytes=48 << 20
        ),
        name="hyena",
    )(*args)


def solution(mesh):
    placed = (
        P("seq"),
        P(None, None, "chan"),
        P(None, None, "chan"),
        P(None, "seq", None, "chan"),
        P("chan", "seq"),
    )
    return jax.shard_map(
        per_device,
        mesh=mesh,
        in_specs=placed,
        out_specs=(P("seq", "chan"), P("seq", "chan")),
        check_vma=False,
    )
```
